32 devices in a mesh: strip: 2 (over x), ifg: 16 (over z, y, core).
Axes of the slice: x: 2, y: 2, z: 4, core: 2. Of those that a mesh axis runs over, the one named last changes fastest.
Arguments:
- phases: bfloat16 [1024, 128, 512], P('ifg', 'strip'), parts along dimension 1, may hold values from -9 to 9
- coherence: int32 [8, 32], P('strip'), parts along dimension 0, may hold values from 0 to 1
- date_pairs: int32 [1024, 2], replicated, may hold values from 0 to 255
- ramp_inverse: bfloat16 [1024, 1024], replicated, as said below
- pseudo_inverse: bfloat16 [256, 1024], replicated, may hold values from -0.1875 to 0.1875
Outputs:
- displacement: float32 [256, 128, 512], P(None, ('strip', 'ifg')), parts along dimension 1
- residual_phase: bfloat16 [1024, 128, 512], P('ifg', 'strip'), parts along dimension 1
The draws below stay inside these ranges and needn't reach their ends.
There are 2 independent parts, one for each index of `strip`. The reference program is written for one: setup_inputs(seed, part) draws one part's arguments, and reference() takes and returns one part's arrays. A program takes and returns all parts, laid end to end along the dimension named above; an argument that names none is the same for every part. Nothing has to cross between parts.
Inputs may be any that keep to these rules, and one draw needn't show every extreme that they name: `ramp_inverse`: full rank.
All inputs are finite; a program needn't handle non-finite values.
Results may differ from the reference program's by a relative error of at most 0.0049.
Values may be sent and summed in bfloat16 or wider, within the bound.
A program may use at most 128 MiB of HBM per device.

```python
import math
import jax
import jax.numpy as jnp
from jax import lax

IFG = 1024
DATES = 256
KNOTS = 32
BLOCK = 16
COLS = 512
ROWS = 64


def draw_phases(key, part):
    keys = jax.random.split(key, 6)
    across = jnp.arange(ROWS, dtype=jnp.float32) / ROWS
    along = jnp.arange(COLS, dtype=jnp.float32) / COLS
    amplitude = jax.random.uniform(keys[0], (IFG, 1, 1), jnp.float32, 1.0, 4.0)
    noise = jnp.clip(jax.random.normal(keys[1], (IFG, ROWS, COLS), jnp.float32), -4.0, 4.0)
    freq_rows = jax.random.uniform(keys[2], (IFG, 1, 1), jnp.float32, -1.5, 1.5)
    freq_cols = jax.random.uniform(keys[3], (IFG, 1, 1), jnp.float32, -1.5, 1.5)
    offset = jax.random.uniform(keys[4], (IFG, 1, 1), jnp.float32, -math.pi, math.pi)
    slope = jax.random.uniform(keys[5], (IFG, 1, 1), jnp.float32, -1.0, 1.0)
    angle_field = 2.0 * math.pi * (freq_rows * across[None, :, None] + freq_cols * along[None, None, :]) + offset
    smooth = amplitude * jnp.cos(angle_field) + slope * (2.0 * across[None, :, None] - 1.0)
    return (smooth + noise).astype(jnp.bfloat16)


def draw_coherence(key, part):
    key = jax.random.fold_in(key, 11)
    keys = jax.random.split(key, 3)
    block_rows = ROWS // BLOCK
    block_cols = COLS // BLOCK
    col_run = max(5 * block_cols // 8, 1)
    row_run = max(block_rows // 4, 1)
    col_start = jax.random.randint(keys[0], (), 0, block_cols - col_run + 1)
    row_start = jax.random.randint(keys[1], (), 0, block_rows - row_run + 1)
    scatter_bits = jax.random.randint(keys[2], (block_rows, block_cols), 0, 4)
    col_index = jnp.arange(block_cols, dtype=jnp.int32)[None, :]
    row_index = jnp.arange(block_rows, dtype=jnp.int32)[:, None]
    in_col_void = (col_index >= col_start) & (col_index < col_start + col_run)
    in_row_void = (row_index >= row_start) & (row_index < row_start + row_run)
    coherent = (scatter_bits < 3) & jnp.logical_not(in_col_void) & jnp.logical_not(in_row_void)
    return jnp.where(coherent, 1, 0).astype(jnp.int32)


def draw_ramp_inverse(key, part):
    key = jax.random.fold_in(key, 23)
    keys = jax.random.split(key, 2)
    square = KNOTS * KNOTS
    pixels = ROWS * COLS / square
    diagonal = jax.random.uniform(keys[0], (square,), jnp.float32, 0.6, 1.0)
    spread = jnp.clip(jax.random.normal(keys[1], (square, square), jnp.float32), -4.0, 4.0)
    matrix = 0.5 * spread / math.sqrt(square) + jnp.eye(square, dtype=jnp.float32) * diagonal[None, :]
    return (matrix / pixels).astype(jnp.bfloat16)


def touch_ends(drawn, own_key, low, top_value):
    longest = drawn.shape.index(max(drawn.shape))
    spots = []
    for shift in (0, 1):
        where = [jax.random.randint(jax.random.fold_in(own_key, axis), (), 0, length) for axis, length in enumerate(drawn.shape)]
        where[longest] = (where[longest] + shift) % drawn.shape[longest]
        spots.append(tuple(where))
    return drawn.at[spots[0]].set(low).at[spots[1]].set(top_value)


def bell_draw(key, extent, scale, limit, held_as=jnp.bfloat16):
    entries = scale * jax.random.normal(key, extent, jnp.float32)
    return jnp.clip(entries, min=-limit, max=limit).astype(held_as)


def setup_inputs(seed: int = 0, part: int = 0) -> dict:
    streams_of = jax.random.split(jax.random.key(seed), 6)
    own_keys = jax.random.split(jax.random.fold_in(streams_of[5], part), 6)
    phases = draw_phases(jax.random.fold_in(jax.random.fold_in(streams_of[5], part), 71), part)
    coherence = draw_coherence(jax.random.fold_in(jax.random.fold_in(streams_of[5], part), 71), part)
    date_pairs = touch_ends(jax.random.randint(streams_of[2], (IFG, 2), 0, DATES), jax.random.fold_in(streams_of[2], 1), 0, DATES - 1).astype(jnp.int32)
    ramp_inverse = draw_ramp_inverse(jax.random.fold_in(streams_of[5], 71), part)
    pseudo_inverse = bell_draw(streams_of[4], (DATES, IFG), IFG ** -0.5, 0.1875)
    return dict(phases=phases, coherence=coherence, date_pairs=date_pairs, ramp_inverse=ramp_inverse, pseudo_inverse=pseudo_inverse)


highest = lax.Precision.HIGHEST


def spline_basis(count, knot_count):
    spacing = (knot_count - 3) / (count - 1)
    places = jnp.arange(count, dtype=jnp.float32) * spacing
    centres = jnp.arange(knot_count, dtype=jnp.float32) - 1.0
    offset = jnp.abs(places[:, None] - centres[None, :])
    inner = 2.0 / 3.0 - offset * offset + 0.5 * offset ** 3
    outer = (2.0 - offset) ** 3 / 6.0
    return jnp.where(offset < 1.0, inner, jnp.where(offset < 2.0, outer, 0.0)).astype(jnp.float32)


def weight_field(coherence):
    block_rows, block_cols = coherence.shape
    spread = jnp.broadcast_to(coherence.astype(jnp.float32)[:, None, :, None], (block_rows, BLOCK, block_cols, BLOCK))
    return spread.reshape(block_rows * BLOCK, block_cols * BLOCK)


def reference(phases, coherence, date_pairs, ramp_inverse, pseudo_inverse):
    row_basis = spline_basis(ROWS, KNOTS)
    col_basis = spline_basis(COLS, KNOTS)
    weight = weight_field(coherence)
    masked = phases.astype(jnp.float32) * weight
    partial_score = jnp.einsum("irc,cb->irb", masked, col_basis, precision=highest)
    score = jnp.einsum("ra,irb->iab", row_basis, partial_score, precision=highest)
    solved = jnp.dot(ramp_inverse.astype(jnp.float32), score.reshape(IFG, KNOTS * KNOTS).T, precision=highest)
    coefficients = solved.T.reshape(IFG, KNOTS, KNOTS)
    ramp_rows = jnp.einsum("ra,iab->irb", row_basis, coefficients, precision=highest)
    ramp = jnp.einsum("irb,cb->irc", ramp_rows, col_basis, precision=highest)
    corrected = (phases.astype(jnp.float32) - ramp).astype(jnp.bfloat16)
    flat = corrected.reshape(IFG, ROWS * COLS)
    displacement = jnp.dot(pseudo_inverse, flat, preferred_element_type=jnp.float32).reshape(DATES, ROWS, COLS)
    modeled = displacement[date_pairs[:, 1]] - displacement[date_pairs[:, 0]]
    residual_phase = (corrected.astype(jnp.float32) - modeled).astype(jnp.bfloat16)
    return (displacement, residual_phase)
```

```python
import functools

import jax
import jax.numpy as jnp
from jax import lax
from jax.experimental import pallas as pl
from jax.experimental.pallas import tpu as pltpu
from jax.sharding import PartitionSpec as P

KNOTS = 32
BLOCK = 16
PLANE = 4
LINE = 4
PARTS = 1

highest = lax.Precision.HIGHEST
f32 = jnp.float32
bf16 = jnp.bfloat16


def spline_basis(count, knot_count):
    spacing = (knot_count - 3) / (count - 1)
    places = jnp.arange(count, dtype=jnp.float32) * spacing
    centres = jnp.arange(knot_count, dtype=jnp.float32) - 1.0
    offset = jnp.abs(places[:, None] - centres[None, :])
    inner = 2.0 / 3.0 - offset * offset + 0.5 * offset**3
    outer = (2.0 - offset) ** 3 / 6.0
    return jnp.where(offset < 1.0, inner, jnp.where(offset < 2.0, outer, 0.0))


def weight_field(coherence):
    block_rows, block_cols = coherence.shape
    spread = jnp.broadcast_to(
        coherence.astype(jnp.float32)[:, None, :, None], (block_rows, BLOCK, block_cols, BLOCK)
    )
    return spread.reshape(block_rows * BLOCK, block_cols * BLOCK)


def fit_ramp(phases, coherence, ramp_inverse):
    local_count, row_count, col_count = phases.shape
    square = KNOTS * KNOTS
    row_basis = spline_basis(row_count, KNOTS)
    col_basis = spline_basis(col_count, KNOTS)
    masked = phases.astype(jnp.float32) * weight_field(coherence)
    partial_score = jnp.einsum("irc,cb->irb", masked, col_basis, precision=highest)
    score = jnp.einsum("ra,irb->iab", row_basis, partial_score, precision=highest)
    solved = jnp.dot(
        ramp_inverse.astype(jnp.float32), score.reshape(local_count, square).T, precision=highest
    )
    return solved.T.reshape(local_count, KNOTS, KNOTS), row_basis, col_basis


def per_device(phases, coherence, date_pairs, ramp_inverse, pseudo_inverse):
    row_count = phases.shape[1]
    row_share = row_count // lax.axis_size("ifg")
    coefficients, row_basis, col_basis = fit_ramp(phases, coherence, ramp_inverse)
    ramp_rows = jnp.einsum("ra,iab->irb", row_basis, coefficients, precision=highest)
    ramp = jnp.einsum("irb,cb->irc", ramp_rows, col_basis, precision=highest)
    payload = (phases.astype(jnp.float32) - ramp).astype(jnp.bfloat16)
    regrouped = lax.all_to_all(payload, "ifg", split_axis=1, concat_axis=0, tiled=True)
    total_count, _, col_count = regrouped.shape
    flat = regrouped.reshape(total_count, row_share * col_count)
    displacement = jnp.dot(pseudo_inverse, flat, preferred_element_type=jnp.float32)
    displacement = displacement.reshape(pseudo_inverse.shape[0], row_share, col_count)
    later = jnp.take(displacement, date_pairs[:, 1], axis=0)
    earlier = jnp.take(displacement, date_pairs[:, 0], axis=0)
    residual_band = (regrouped.astype(jnp.float32) - (later - earlier)).astype(jnp.bfloat16)
    residual_phase = lax.all_to_all(residual_band, "ifg", split_axis=0, concat_axis=1, tiled=True)
    return (displacement, residual_phase)


def line_kernel(
    corr, own_ref, out_ref, pair_ref, disp, resid,
    raw, near, far, mid_send, back_send, res_send,
    raw_ss, raw_rs, near_ss, near_rs, far_ss, far_rs, res_ss, res_rs,
):
    rows, count, cols = corr.shape
    chunks, total_count, width = raw.shape
    share = rows // (PLANE * LINE)
    me = lax.axis_index("ifg")
    z = me // PLANE
    q = me % PLANE
    side = z // 2
    inner_z = 1 + side
    outer_z = 3 * side
    is_inner = (z - outer_z) * (1 - 2 * side)
    beside = (inner_z + outer_z - z) * PLANE + q
    partner = (LINE - 1 - z) * PLANE + q
    MESH = pl.DeviceIdType.MESH

    def place(k, owner):
        row = k // PARTS
        return (row // share) * share * PLANE + owner * share + row % share, (k % PARTS) * width

    def peer(p):
        return (q + p) % PLANE

    def source(p):
        return (q + PLANE - p) % PLANE

    def raw_copy(k, p):
        row, col = place(k, peer(p))
        return pltpu.make_async_remote_copy(
            src_ref=corr.at[row, :, pl.ds(pl.multiple_of(col, width), width)],
            dst_ref=raw.at[k, pl.ds(pl.multiple_of(q * count, count), count), :],
            send_sem=raw_ss.at[k, p - 1], recv_sem=raw_rs.at[k, p - 1],
            device_id={"ifg": z * PLANE + peer(p)}, device_id_type=MESH)

    def res_copy(k, p):
        row, col = place(k, q)
        return pltpu.make_async_remote_copy(
            src_ref=res_send.at[k, pl.ds(pl.multiple_of(peer(p) * count, count), count), :],
            dst_ref=resid.at[row, :, pl.ds(pl.multiple_of(col, width), width)],
            send_sem=res_ss.at[k, p - 1], recv_sem=res_rs.at[k, p - 1],
            device_id={"ifg": z * PLANE + peer(p)}, device_id_type=MESH)

    def line_copy(src, dst, ss, rs, k, target):
        return pltpu.make_async_remote_copy(
            src_ref=src.at[k], dst_ref=dst.at[k], send_sem=ss.at[k], recv_sem=rs.at[k],
            device_id={"ifg": target}, device_id_type=MESH)

    barrier = pltpu.get_barrier_semaphore()
    for p in range(1, PLANE):
        pl.semaphore_signal(
            barrier, inc=1, device_id={"ifg": z * PLANE + peer(p)}, device_id_type=MESH)
    pl.semaphore_signal(barrier, inc=1, device_id={"ifg": beside}, device_id_type=MESH)

    @pl.when(is_inner == 1)
    def _():
        pl.semaphore_signal(barrier, inc=1, device_id={"ifg": partner}, device_id_type=MESH)

    pl.semaphore_wait(barrier, PLANE + is_inner)

    @pl.loop(0, chunks)
    def _(k):
        for p in range(1, PLANE):
            raw_copy(k, p).start()

    def dot(a, b):
        return jnp.dot(a, b, preferred_element_type=f32)

    def finish(k, total):
        row, col = place(k, q)

        @pl.when((k // PARTS) // share == z)
        def _():
            disp[(k // PARTS) % share, :, pl.ds(pl.multiple_of(col, width), width)] = total

        high = total.astype(bf16)
        low = (total - high.astype(f32)).astype(bf16)
        modeled = dot(pair_ref[...], high) + dot(pair_ref[...], low)
        res_send[k] = (raw[k].astype(f32) - modeled).astype(bf16)
        for p in range(1, PLANE):
            res_copy(k, p).start()
        resid[row, :, pl.ds(pl.multiple_of(col, width), width)] = res_send[
            k, pl.ds(pl.multiple_of(q * count, count), count), :]

    @pl.loop(0, chunks + 4)
    def _(t):
        @pl.when(t < chunks)
        def _():
            k = t
            row, col = place(k, q)
            raw[k, pl.ds(pl.multiple_of(q * count, count), count), :] = corr[
                row, :, pl.ds(pl.multiple_of(col, width), width)]
            for p in range(1, PLANE):
                raw_copy(k, p).wait_recv()

            @pl.when(is_inner == 0)
            def _():
                line_copy(raw, near, near_ss, near_rs, k, beside).start()

            @pl.when(is_inner == 1)
            def _():
                line_copy(raw, near, near_ss, near_rs, k, beside).wait_recv()
                half = dot(out_ref[...], near[k]) + dot(own_ref[...], raw[k])
                mid_send[k] = half.astype(bf16)
                line_copy(mid_send, far, far_ss.at[0], far_rs, k, partner).start()

        @pl.when((is_inner == 1) & (t >= 2) & (t < chunks + 2))
        def _():
            k = t - 2
            line_copy(mid_send, far, far_ss.at[0], far_rs, k, partner).wait_recv()
            rest = far[k].astype(f32) + dot(own_ref[...], raw[k])
            back_send[k] = rest.astype(bf16)
            line_copy(back_send, far, far_ss.at[1], far_rs, k, beside).start()
            finish(k, rest + dot(out_ref[...], near[k]))

        @pl.when((is_inner == 0) & (t >= 4))
        def _():
            k = t - 4
            line_copy(back_send, far, far_ss.at[1], far_rs, k, beside).wait_recv()
            finish(k, far[k].astype(f32) + dot(own_ref[...], raw[k]))

    @pl.loop(0, chunks)
    def _(k):
        for p in range(1, PLANE):
            raw_copy(k, p).wait_send()
            res_copy(k, p).wait_send()
            res_copy(k, p).wait_recv()

        @pl.when(is_inner == 0)
        def _():
            line_copy(raw, near, near_ss, near_rs, k, beside).wait_send()

        @pl.when(is_inner == 1)
        def _():
            line_copy(mid_send, far, far_ss.at[0], far_rs, k, partner).wait_send()
            line_copy(back_send, far, far_ss.at[1], far_rs, k, beside).wait_send()


def line_call(corrected, own, outer, pair):
    rows, count, cols = corrected.shape
    dates, total_count = own.shape
    chunks = rows // PLANE * PARTS
    width = cols // PARTS
    share = rows // (PLANE * LINE)
    slots = pltpu.VMEM((chunks, dates, width), bf16)
    sems = pltpu.SemaphoreType.DMA
    vmem = pl.BlockSpec(memory_space=pltpu.VMEM)
    return pl.pallas_call(
        line_kernel,
        out_shape=(
            jax.ShapeDtypeStruct((share, dates, cols), f32),
            jax.ShapeDtypeStruct((rows, count, cols), bf16),
        ),
        in_specs=[vmem] * 4,
        out_specs=(vmem, vmem),
        scratch_shapes=[slots] * 6 + [
            sems((chunks, PLANE - 1)), sems((chunks, PLANE - 1)),
            sems((chunks,)), sems((chunks,)),
            sems((2, chunks)), sems((chunks,)),
            sems((chunks, PLANE - 1)), sems((chunks, PLANE - 1)),
        ],
        compiler_params=pltpu.CompilerParams(
            collective_id=0, has_side_effects=True, vmem_limit_bytes=52 * 2**20),
        name="line_sums",
    )(corrected, own, outer, pair)


def per_device_line(phases, coherence, date_pairs, ramp_inverse, pseudo_inverse):
    dates, ifg_count = pseudo_inverse.shape
    plane_count = ifg_count // LINE
    z = lax.axis_index("ifg") // PLANE
    own = lax.dynamic_slice_in_dim(pseudo_inverse, z * plane_count, plane_count, 1)
    outer = lax.dynamic_slice_in_dim(pseudo_inverse, (z // 2) * 3 * plane_count, plane_count, 1)
    pairs = lax.dynamic_slice_in_dim(date_pairs, z * plane_count, plane_count, 0)
    numbers = jnp.arange(dates, dtype=jnp.int32)[None, :]
    pair = ((pairs[:, 1:] == numbers).astype(f32) - (pairs[:, :1] == numbers).astype(f32)).astype(bf16)
    coefficients, row_basis, col_basis = fit_ramp(phases, coherence, ramp_inverse)
    ramp_rows = jnp.einsum("ra,iab->rib", row_basis, coefficients, precision=highest)
    ramp = jnp.einsum("rib,cb->ric", ramp_rows, col_basis, precision=highest)
    corrected = (phases.transpose(1, 0, 2).astype(f32) - ramp).astype(bf16)
    displacement, residual = line_call(corrected, own, outer, pair)
    return displacement.transpose(1, 0, 2), residual.transpose(1, 0, 2)


def solution(mesh):
    placed = (P("ifg", "strip", None), P("strip", None), P(), P(), P())
    on_line = mesh.shape["ifg"] == PLANE * LINE

    def run(phases, coherence, date_pairs, ramp_inverse, pseudo_inverse):
        dates, ifg_count = pseudo_inverse.shape
        fits = on_line and dates == ifg_count // LINE
        return jax.shard_map(
            per_device_line if fits else per_device,
            mesh=mesh,
            in_specs=placed,
            out_specs=(P(None, ("strip", "ifg"), None), P("ifg", "strip", None)),
            check_vma=False,
        )(phases, coherence, date_pairs, ramp_inverse, pseudo_inverse)

    return run
```

```python
import functools

import jax
import jax.numpy as jnp
from jax import lax
from jax.experimental import pallas as pl
from jax.experimental.pallas import tpu as pltpu
from jax.sharding import PartitionSpec as P

KNOTS = 32
BLOCK = 16
PLANE = 4
LINE = 4
PARTS = 1
LEAD = 3
SKEW = 2

highest = lax.Precision.HIGHEST
f32 = jnp.float32
bf16 = jnp.bfloat16


def spline_basis(count, knot_count):
    spacing = (knot_count - 3) / (count - 1)
    places = jnp.arange(count, dtype=jnp.float32) * spacing
    centres = jnp.arange(knot_count, dtype=jnp.float32) - 1.0
    offset = jnp.abs(places[:, None] - centres[None, :])
    inner = 2.0 / 3.0 - offset * offset + 0.5 * offset**3
    outer = (2.0 - offset) ** 3 / 6.0
    return jnp.where(offset < 1.0, inner, jnp.where(offset < 2.0, outer, 0.0))


def weight_field(coherence):
    block_rows, block_cols = coherence.shape
    spread = jnp.broadcast_to(
        coherence.astype(jnp.float32)[:, None, :, None], (block_rows, BLOCK, block_cols, BLOCK)
    )
    return spread.reshape(block_rows * BLOCK, block_cols * BLOCK)


def fit_ramp(phases, coherence, ramp_inverse):
    local_count, row_count, col_count = phases.shape
    square = KNOTS * KNOTS
    row_basis = spline_basis(row_count, KNOTS)
    col_basis = spline_basis(col_count, KNOTS)
    masked = phases.astype(jnp.float32) * weight_field(coherence)
    partial_score = jnp.einsum("irc,cb->irb", masked, col_basis, precision=highest)
    score = jnp.einsum("ra,irb->iab", row_basis, partial_score, precision=highest)
    solved = jnp.dot(
        ramp_inverse.astype(jnp.float32), score.reshape(local_count, square).T, precision=highest
    )
    return solved.T.reshape(local_count, KNOTS, KNOTS), row_basis, col_basis


def per_device(phases, coherence, date_pairs, ramp_inverse, pseudo_inverse):
    row_count = phases.shape[1]
    row_share = row_count // lax.axis_size("ifg")
    coefficients, row_basis, col_basis = fit_ramp(phases, coherence, ramp_inverse)
    ramp_rows = jnp.einsum("ra,iab->irb", row_basis, coefficients, precision=highest)
    ramp = jnp.einsum("irb,cb->irc", ramp_rows, col_basis, precision=highest)
    payload = (phases.astype(jnp.float32) - ramp).astype(jnp.bfloat16)
    regrouped = lax.all_to_all(payload, "ifg", split_axis=1, concat_axis=0, tiled=True)
    total_count, _, col_count = regrouped.shape
    flat = regrouped.reshape(total_count, row_share * col_count)
    displacement = jnp.dot(pseudo_inverse, flat, preferred_element_type=jnp.float32)
    displacement = displacement.reshape(pseudo_inverse.shape[0], row_share, col_count)
    later = jnp.take(displacement, date_pairs[:, 1], axis=0)
    earlier = jnp.take(displacement, date_pairs[:, 0], axis=0)
    residual_band = (regrouped.astype(jnp.float32) - (later - earlier)).astype(jnp.bfloat16)
    residual_phase = lax.all_to_all(residual_band, "ifg", split_axis=0, concat_axis=1, tiled=True)
    return (displacement, residual_phase)


def line_kernel(
    phase_ref, ramp_ref, basis_ref, own_ref, out_ref, pair_ref, disp, resid,
    corr, raw, near, far, mid_send, back_send, res_send,
    raw_ss, raw_rs, near_ss, near_rs, far_ss, far_rs, res_ss, res_rs,
):
    rows, count, cols = phase_ref.shape
    chunks, total_count, width = raw.shape
    share = rows // (PLANE * LINE)
    me = lax.axis_index("ifg")
    z = me // PLANE
    q = me % PLANE
    side = z // 2
    inner_z = 1 + side
    outer_z = 3 * side
    is_inner = (z - outer_z) * (1 - 2 * side)
    beside = (inner_z + outer_z - z) * PLANE + q
    partner = (LINE - 1 - z) * PLANE + q
    MESH = pl.DeviceIdType.MESH

    def place(k, owner):
        row = k // PARTS
        return (row // share) * share * PLANE + owner * share + row % share, (k % PARTS) * width

    def peer(p):
        return (q + p) % PLANE

    def raw_copy(k, p):
        return pltpu.make_async_remote_copy(
            src_ref=corr.at[k, p - 1],
            dst_ref=raw.at[k, pl.ds(pl.multiple_of(q * count, count), count), :],
            send_sem=raw_ss.at[k, p - 1], recv_sem=raw_rs.at[k, p - 1],
            device_id={"ifg": z * PLANE + peer(p)}, device_id_type=MESH)

    def res_copy(k, p):
        row, col = place(k, q)
        return pltpu.make_async_remote_copy(
            src_ref=res_send.at[k, pl.ds(pl.multiple_of(peer(p) * count, count), count), :],
            dst_ref=resid.at[row, :, pl.ds(pl.multiple_of(col, width), width)],
            send_sem=res_ss.at[k, p - 1], recv_sem=res_rs.at[k, p - 1],
            device_id={"ifg": z * PLANE + peer(p)}, device_id_type=MESH)

    def line_copy(src, dst, ss, rs, k, target):
        return pltpu.make_async_remote_copy(
            src_ref=src.at[k], dst_ref=dst.at[k], send_sem=ss.at[k], recv_sem=rs.at[k],
            device_id={"ifg": target}, device_id_type=MESH)

    barrier = pltpu.get_barrier_semaphore()
    for p in range(1, PLANE):
        pl.semaphore_signal(
            barrier, inc=1, device_id={"ifg": z * PLANE + peer(p)}, device_id_type=MESH)
    pl.semaphore_signal(barrier, inc=1, device_id={"ifg": beside}, device_id_type=MESH)

    @pl.when(is_inner == 1)
    def _():
        pl.semaphore_signal(barrier, inc=1, device_id={"ifg": partner}, device_id_type=MESH)

    pl.semaphore_wait(barrier, PLANE + is_inner)

    def dot(a, b):
        return jnp.dot(a, b, preferred_element_type=f32)

    def produce(k):
        for p in range(1, PLANE + 1):
            row, col = place(k, peer(p))
            part = pl.ds(pl.multiple_of(col, width), width)
            ramp = dot(ramp_ref[row], basis_ref[:, part])
            corrected = (phase_ref[row, :, part].astype(f32) - ramp).astype(bf16)
            if p == PLANE:
                raw[k, pl.ds(pl.multiple_of(q * count, count), count), :] = corrected
            else:
                corr[k, p - 1] = corrected
                raw_copy(k, p).start()

    @pl.loop(0, LEAD)
    def _(k):
        produce(k)

    def finish(k, total):
        row, col = place(k, q)

        @pl.when((k // PARTS) // share == z)
        def _():
            disp[(k // PARTS) % share, :, pl.ds(pl.multiple_of(col, width), width)] = total

        high = total.astype(bf16)
        low = (total - high.astype(f32)).astype(bf16)
        modeled = dot(pair_ref[...], high) + dot(pair_ref[...], low)
        res_send[k] = (raw[k].astype(f32) - modeled).astype(bf16)
        for p in range(1, PLANE):
            res_copy(k, p).start()
        resid[row, :, pl.ds(pl.multiple_of(col, width), width)] = res_send[
            k, pl.ds(pl.multiple_of(q * count, count), count), :]

    @pl.loop(0, chunks + 2 * SKEW)
    def _(t):
        @pl.when(t + LEAD < chunks)
        def _():
            produce(t + LEAD)

        @pl.when(t < chunks)
        def _():
            k = t
            for p in range(1, PLANE):
                raw_copy(k, p).wait_recv()

            @pl.when(is_inner == 0)
            def _():
                line_copy(raw, near, near_ss, near_rs, k, beside).start()

            @pl.when(is_inner == 1)
            def _():
                line_copy(raw, near, near_ss, near_rs, k, beside).wait_recv()
                half = dot(out_ref[...], near[k]) + dot(own_ref[...], raw[k])
                mid_send[k] = half.astype(bf16)
                line_copy(mid_send, far, far_ss.at[0], far_rs, k, partner).start()

        @pl.when((is_inner == 1) & (t >= SKEW) & (t < chunks + SKEW))
        def _():
            k = t - SKEW
            line_copy(mid_send, far, far_ss.at[0], far_rs, k, partner).wait_recv()
            rest = far[k].astype(f32) + dot(own_ref[...], raw[k])
            back_send[k] = rest.astype(bf16)
            line_copy(back_send, far, far_ss.at[1], far_rs, k, beside).start()
            finish(k, rest + dot(out_ref[...], near[k]))

        @pl.when((is_inner == 0) & (t >= 2 * SKEW))
        def _():
            k = t - 2 * SKEW
            line_copy(back_send, far, far_ss.at[1], far_rs, k, beside).wait_recv()
            finish(k, far[k].astype(f32) + dot(own_ref[...], raw[k]))

    @pl.loop(0, chunks)
    def _(k):
        for p in range(1, PLANE):
            raw_copy(k, p).wait_send()
            res_copy(k, p).wait_send()
            res_copy(k, p).wait_recv()

        @pl.when(is_inner == 0)
        def _():
            line_copy(raw, near, near_ss, near_rs, k, beside).wait_send()

        @pl.when(is_inner == 1)
        def _():
            line_copy(mid_send, far, far_ss.at[0], far_rs, k, partner).wait_send()
            line_copy(back_send, far, far_ss.at[1], far_rs, k, beside).wait_send()


def line_call(phases, ramp_rows, basis, own, outer, pair):
    rows, count, cols = phases.shape
    dates, total_count = own.shape
    chunks = rows // PLANE * PARTS
    width = cols // PARTS
    share = rows // (PLANE * LINE)
    slots = pltpu.VMEM((chunks, dates, width), bf16)
    sems = pltpu.SemaphoreType.DMA
    vmem = pl.BlockSpec(memory_space=pltpu.VMEM)
    return pl.pallas_call(
        line_kernel,
        out_shape=(
            jax.ShapeDtypeStruct((share, dates, cols), f32),
            jax.ShapeDtypeStruct((rows, count, cols), bf16),
        ),
        in_specs=[vmem] * 6,
        out_specs=(vmem, vmem),
        scratch_shapes=[pltpu.VMEM((chunks, PLANE - 1, count, width), bf16)] + [slots] * 6 + [
            sems((chunks, PLANE - 1)), sems((chunks, PLANE - 1)),
            sems((chunks,)), sems((chunks,)),
            sems((2, chunks)), sems((chunks,)),
            sems((chunks, PLANE - 1)), sems((chunks, PLANE - 1)),
        ],
        compiler_params=pltpu.CompilerParams(
            collective_id=0, has_side_effects=True, vmem_limit_bytes=52 * 2**20),
        name="line_sums",
    )(phases, ramp_rows, basis, own, outer, pair)


def split(values):
    high = values.astype(bf16)
    return high, (values - high.astype(f32)).astype(bf16)


def per_device_line(phases, coherence, date_pairs, ramp_inverse, pseudo_inverse):
    dates, ifg_count = pseudo_inverse.shape
    plane_count = ifg_count // LINE
    z = lax.axis_index("ifg") // PLANE
    own = lax.dynamic_slice_in_dim(pseudo_inverse, z * plane_count, plane_count, 1)
    outer = lax.dynamic_slice_in_dim(pseudo_inverse, (z // 2) * 3 * plane_count, plane_count, 1)
    pairs = lax.dynamic_slice_in_dim(date_pairs, z * plane_count, plane_count, 0)
    numbers = jnp.arange(dates, dtype=jnp.int32)[None, :]
    pair = ((pairs[:, 1:] == numbers).astype(f32) - (pairs[:, :1] == numbers).astype(f32)).astype(bf16)
    local_count, row_count, col_count = phases.shape
    row_basis = spline_basis(row_count, KNOTS)
    col_basis = spline_basis(col_count, KNOTS)
    high, low = split(col_basis)
    masked = jnp.where(weight_field(coherence) > 0, phases, jnp.zeros_like(phases))
    halves = jnp.einsum(
        "irc,cb->irb", masked, jnp.concatenate([high, low], 1), preferred_element_type=f32)
    partial_score = halves[:, :, :KNOTS] + halves[:, :, KNOTS:]
    score = jnp.einsum("ra,irb->iab", row_basis, partial_score, precision=highest)
    coefficients = jnp.dot(
        ramp_inverse.astype(f32), score.reshape(local_count, -1).T, precision=highest
    ).T.reshape(local_count, KNOTS, KNOTS)
    ramp_rows = jnp.einsum("ra,iab->rib", row_basis, coefficients, precision=highest)
    rows_high, rows_low = split(ramp_rows)
    displacement, residual = line_call(
        phases.transpose(1, 0, 2),
        jnp.concatenate([rows_high, rows_high, rows_low], 2),
        jnp.concatenate([high, low, high], 1).T,
        own, outer, pair)
    return displacement.transpose(1, 0, 2), residual.transpose(1, 0, 2)


def solution(mesh):
    placed = (P("ifg", "strip", None), P("strip", None), P(), P(), P())
    on_line = mesh.shape["ifg"] == PLANE * LINE

    def run(phases, coherence, date_pairs, ramp_inverse, pseudo_inverse):
        dates, ifg_count = pseudo_inverse.shape
        fits = on_line and dates == ifg_count // LINE
        return jax.shard_map(
            per_device_line if fits else per_device,
            mesh=mesh,
            in_specs=placed,
            out_specs=(P(None, ("strip", "ifg"), None), P("ifg", "strip", None)),
            check_vma=False,
        )(phases, coherence, date_pairs, ramp_inverse, pseudo_inverse)

    return run
```

```python
import functools

import jax
import jax.numpy as jnp
from jax import lax
from jax.experimental import pallas as pl
from jax.experimental.pallas import tpu as pltpu
from jax.sharding import PartitionSpec as P

KNOTS = 32
BLOCK = 16
PLANE = 4
LINE = 4
PARTS = 2
LEAD = 4
SKEW = 3

highest = lax.Precision.HIGHEST
f32 = jnp.float32
bf16 = jnp.bfloat16


def spline_basis(count, knot_count):
    spacing = (knot_count - 3) / (count - 1)
    places = jnp.arange(count, dtype=jnp.float32) * spacing
    centres = jnp.arange(knot_count, dtype=jnp.float32) - 1.0
    offset = jnp.abs(places[:, None] - centres[None, :])
    inner = 2.0 / 3.0 - offset * offset + 0.5 * offset**3
    outer = (2.0 - offset) ** 3 / 6.0
    return jnp.where(offset < 1.0, inner, jnp.where(offset < 2.0, outer, 0.0))


def weight_field(coherence):
    block_rows, block_cols = coherence.shape
    spread = jnp.broadcast_to(
        coherence.astype(jnp.float32)[:, None, :, None], (block_rows, BLOCK, block_cols, BLOCK)
    )
    return spread.reshape(block_rows * BLOCK, block_cols * BLOCK)


def fit_ramp(phases, coherence, ramp_inverse):
    local_count, row_count, col_count = phases.shape
    square = KNOTS * KNOTS
    row_basis = spline_basis(row_count, KNOTS)
    col_basis = spline_basis(col_count, KNOTS)
    masked = phases.astype(jnp.float32) * weight_field(coherence)
    partial_score = jnp.einsum("irc,cb->irb", masked, col_basis, precision=highest)
    score = jnp.einsum("ra,irb->iab", row_basis, partial_score, precision=highest)
    solved = jnp.dot(
        ramp_inverse.astype(jnp.float32), score.reshape(local_count, square).T, precision=highest
    )
    return solved.T.reshape(local_count, KNOTS, KNOTS), row_basis, col_basis


def per_device(phases, coherence, date_pairs, ramp_inverse, pseudo_inverse):
    row_count = phases.shape[1]
    row_share = row_count // lax.axis_size("ifg")
    coefficients, row_basis, col_basis = fit_ramp(phases, coherence, ramp_inverse)
    ramp_rows = jnp.einsum("ra,iab->irb", row_basis, coefficients, precision=highest)
    ramp = jnp.einsum("irb,cb->irc", ramp_rows, col_basis, precision=highest)
    payload = (phases.astype(jnp.float32) - ramp).astype(jnp.bfloat16)
    regrouped = lax.all_to_all(payload, "ifg", split_axis=1, concat_axis=0, tiled=True)
    total_count, _, col_count = regrouped.shape
    flat = regrouped.reshape(total_count, row_share * col_count)
    displacement = jnp.dot(pseudo_inverse, flat, preferred_element_type=jnp.float32)
    displacement = displacement.reshape(pseudo_inverse.shape[0], row_share, col_count)
    later = jnp.take(displacement, date_pairs[:, 1], axis=0)
    earlier = jnp.take(displacement, date_pairs[:, 0], axis=0)
    residual_band = (regrouped.astype(jnp.float32) - (later - earlier)).astype(jnp.bfloat16)
    residual_phase = lax.all_to_all(residual_band, "ifg", split_axis=0, concat_axis=1, tiled=True)
    return (displacement, residual_phase)


def line_kernel(
    phase_ref, ramp_ref, basis_ref, own_ref, out_ref, pair_ref, disp, resid,
    corr, own_part, out_part, raw, near, far, mid_send, back_send, res_send,
    raw_ss, raw_rs, near_ss, near_rs, far_ss, far_rs, res_ss, res_rs,
):
    rows, count, cols = phase_ref.shape
    chunks, total_count, width = raw.shape
    share = rows // (PLANE * LINE)
    me = lax.axis_index("ifg")
    z = me // PLANE
    q = me % PLANE
    side = z // 2
    inner_z = 1 + side
    outer_z = 3 * side
    is_inner = (z - outer_z) * (1 - 2 * side)
    beside = (inner_z + outer_z - z) * PLANE + q
    partner = (LINE - 1 - z) * PLANE + q
    MESH = pl.DeviceIdType.MESH

    def place(k, owner):
        row = k // PARTS
        return (row // share) * share * PLANE + owner * share + row % share, (k % PARTS) * width

    def peer(p):
        return (q + p) % PLANE

    def raw_copy(k, p):
        return pltpu.make_async_remote_copy(
            src_ref=corr.at[k, p - 1],
            dst_ref=raw.at[k, pl.ds(pl.multiple_of(q * count, count), count), :],
            send_sem=raw_ss.at[k, p - 1], recv_sem=raw_rs.at[k, p - 1],
            device_id={"ifg": z * PLANE + peer(p)}, device_id_type=MESH)

    def res_copy(k, p):
        row, col = place(k, q)
        return pltpu.make_async_remote_copy(
            src_ref=res_send.at[k, pl.ds(pl.multiple_of(peer(p) * count, count), count), :],
            dst_ref=resid.at[row, :, pl.ds(pl.multiple_of(col, width), width)],
            send_sem=res_ss.at[k, p - 1], recv_sem=res_rs.at[k, p - 1],
            device_id={"ifg": z * PLANE + peer(p)}, device_id_type=MESH)

    def line_copy(src, dst, ss, rs, k, target):
        return pltpu.make_async_remote_copy(
            src_ref=src.at[k], dst_ref=dst.at[k], send_sem=ss.at[k], recv_sem=rs.at[k],
            device_id={"ifg": target}, device_id_type=MESH)

    barrier = pltpu.get_barrier_semaphore()
    for p in range(1, PLANE):
        pl.semaphore_signal(
            barrier, inc=1, device_id={"ifg": z * PLANE + peer(p)}, device_id_type=MESH)
    pl.semaphore_signal(barrier, inc=1, device_id={"ifg": beside}, device_id_type=MESH)

    @pl.when(is_inner == 1)
    def _():
        pl.semaphore_signal(barrier, inc=1, device_id={"ifg": partner}, device_id_type=MESH)

    pl.semaphore_wait(barrier, PLANE + is_inner)

    def dot(a, b):
        return jnp.dot(a, b, preferred_element_type=f32)

    def produce(k):
        for p in range(1, PLANE + 1):
            row, col = place(k, peer(p))
            part = pl.ds(pl.multiple_of(col, width), width)
            ramp = dot(ramp_ref[row], basis_ref[:, part])
            corrected = (phase_ref[row, :, part].astype(f32) - ramp).astype(bf16)
            if p == PLANE:
                raw[k, pl.ds(pl.multiple_of(q * count, count), count), :] = corrected
            else:
                corr[k, p - 1] = corrected
                raw_copy(k, p).start()

    @pl.loop(0, LEAD)
    def _(k):
        produce(k)

    def finish(k, total):
        row, col = place(k, q)

        @pl.when((k // PARTS) // share == z)
        def _():
            disp[(k // PARTS) % share, :, pl.ds(pl.multiple_of(col, width), width)] = total

        high = total.astype(bf16)
        low = (total - high.astype(f32)).astype(bf16)
        modeled = dot(pair_ref[...], high) + dot(pair_ref[...], low)
        res_send[k] = (raw[k].astype(f32) - modeled).astype(bf16)
        for p in range(1, PLANE):
            res_copy(k, p).start()
        resid[row, :, pl.ds(pl.multiple_of(col, width), width)] = res_send[
            k, pl.ds(pl.multiple_of(q * count, count), count), :]

    @pl.loop(0, chunks + 2 * SKEW)
    def _(t):
        @pl.when(t + LEAD < chunks)
        def _():
            produce(t + LEAD)

        @pl.when(t < chunks)
        def _():
            k = t
            for p in range(1, PLANE):
                raw_copy(k, p).wait_recv()

            @pl.when(is_inner == 0)
            def _():
                line_copy(raw, near, near_ss, near_rs, k, beside).start()

            @pl.when(is_inner == 1)
            def _():
                line_copy(raw, near, near_ss, near_rs, k, beside).wait_recv()
                slot = k % (SKEW + 1)
                own_sum = dot(own_ref[...], raw[k])
                out_sum = dot(out_ref[...], near[k])
                own_part[slot] = own_sum
                out_part[slot] = out_sum
                mid_send[k] = (own_sum + out_sum).astype(bf16)
                line_copy(mid_send, far, far_ss.at[0], far_rs, k, partner).start()

        @pl.when((is_inner == 1) & (t >= SKEW) & (t < chunks + SKEW))
        def _():
            k = t - SKEW
            line_copy(mid_send, far, far_ss.at[0], far_rs, k, partner).wait_recv()
            slot = k % (SKEW + 1)
            rest = far[k].astype(f32) + own_part[slot]
            back_send[k] = rest.astype(bf16)
            line_copy(back_send, far, far_ss.at[1], far_rs, k, beside).start()
            finish(k, rest + out_part[slot])

        @pl.when((is_inner == 0) & (t >= 2 * SKEW))
        def _():
            k = t - 2 * SKEW
            line_copy(back_send, far, far_ss.at[1], far_rs, k, beside).wait_recv()
            finish(k, far[k].astype(f32) + dot(own_ref[...], raw[k]))

    @pl.loop(0, chunks)
    def _(k):
        for p in range(1, PLANE):
            raw_copy(k, p).wait_send()
            res_copy(k, p).wait_send()
            res_copy(k, p).wait_recv()

        @pl.when(is_inner == 0)
        def _():
            line_copy(raw, near, near_ss, near_rs, k, beside).wait_send()

        @pl.when(is_inner == 1)
        def _():
            line_copy(mid_send, far, far_ss.at[0], far_rs, k, partner).wait_send()
            line_copy(back_send, far, far_ss.at[1], far_rs, k, beside).wait_send()


def line_call(phases, ramp_rows, basis, own, outer, pair):
    rows, count, cols = phases.shape
    dates, total_count = own.shape
    chunks = rows // PLANE * PARTS
    width = cols // PARTS
    share = rows // (PLANE * LINE)
    slots = pltpu.VMEM((chunks, dates, width), bf16)
    sems = pltpu.SemaphoreType.DMA
    vmem = pl.BlockSpec(memory_space=pltpu.VMEM)
    return pl.pallas_call(
        line_kernel,
        out_shape=(
            jax.ShapeDtypeStruct((share, dates, cols), f32),
            jax.ShapeDtypeStruct((rows, count, cols), bf16),
        ),
        in_specs=[vmem] * 6,
        out_specs=(vmem, vmem),
        scratch_shapes=[pltpu.VMEM((chunks, PLANE - 1, count, width), bf16)] + [pltpu.VMEM((SKEW + 1, dates, width), f32)] * 2 + [slots] * 6 + [
            sems((chunks, PLANE - 1)), sems((chunks, PLANE - 1)),
            sems((chunks,)), sems((chunks,)),
            sems((2, chunks)), sems((chunks,)),
            sems((chunks, PLANE - 1)), sems((chunks, PLANE - 1)),
        ],
        compiler_params=pltpu.CompilerParams(
            collective_id=0, has_side_effects=True, vmem_limit_bytes=52 * 2**20),
        name="line_sums",
    )(phases, ramp_rows, basis, own, outer, pair)


def ramp_kernel(
    phase_ref, weight_ref, basis_ref, inverse_ref, row_ref, rows_out, score, flat, coef,
):
    rows, count, cols = phase_ref.shape
    group = 4

    def first(r):
        return jnp.minimum((r * (KNOTS - 3)) // (rows - 1), KNOTS - 4)

    score[...] = jnp.zeros_like(score)

    @pl.loop(0, rows // group)
    def _(g):
        r0 = g * group
        masked = phase_ref[pl.ds(r0, group)] * weight_ref[pl.ds(r0, group)]
        both = jnp.dot(
            masked.reshape(group * count, cols), basis_ref[...], preferred_element_type=f32)
        part = both[:, :KNOTS] + both[:, KNOTS:]
        for j in range(group):
            base = first(r0 + j)
            for d in range(4):
                score[base + d] += row_ref[r0 + j, base + d] * part[j * count:(j + 1) * count]

    for a in range(KNOTS):
        flat[:, a * KNOTS:(a + 1) * KNOTS] = score[a]
    high = flat[...].astype(bf16)
    low = (flat[...] - high.astype(f32)).astype(bf16)
    across = (((1,), (1,)), ((), ()))
    flat[...] = lax.dot_general(
        high, inverse_ref[...], across, preferred_element_type=f32
    ) + lax.dot_general(low, inverse_ref[...], across, preferred_element_type=f32)
    for a in range(KNOTS):
        coef[a] = flat[:, a * KNOTS:(a + 1) * KNOTS]

    @pl.loop(0, rows // group)
    def _(g):
        for j in range(group):
            r = g * group + j
            base = first(r)
            line = row_ref[r, base] * coef[base]
            for d in range(1, 4):
                line += row_ref[r, base + d] * coef[base + d]
            top = line.astype(bf16)
            rest = (line - top.astype(f32)).astype(bf16)
            rows_out[r] = jnp.concatenate([top, top, rest], 1)


def ramp_call(by_row, weight, basis, ramp_inverse, row_basis):
    rows, count, cols = by_row.shape
    vmem = pl.BlockSpec(memory_space=pltpu.VMEM)
    return pl.pallas_call(
        ramp_kernel,
        out_shape=jax.ShapeDtypeStruct((rows, count, 3 * KNOTS), bf16),
        in_specs=[vmem] * 4 + [pl.BlockSpec(memory_space=pltpu.SMEM)],
        out_specs=vmem,
        scratch_shapes=[
            pltpu.VMEM((KNOTS, count, KNOTS), f32),
            pltpu.VMEM((count, KNOTS * KNOTS), f32),
            pltpu.VMEM((KNOTS, count, KNOTS), f32),
        ],
        compiler_params=pltpu.CompilerParams(vmem_limit_bytes=32 * 2**20),
        name="ramp_fit",
    )(by_row, weight, basis, ramp_inverse, row_basis)


def split(values):
    high = lax.reduce_precision(values, exponent_bits=8, mantissa_bits=7)
    return high.astype(bf16), (values - high).astype(bf16)


def per_device_line(phases, coherence, date_pairs, ramp_inverse, pseudo_inverse):
    dates, ifg_count = pseudo_inverse.shape
    plane_count = ifg_count // LINE
    z = lax.axis_index("ifg") // PLANE
    own = lax.dynamic_slice_in_dim(pseudo_inverse, z * plane_count, plane_count, 1)
    outer = lax.dynamic_slice_in_dim(pseudo_inverse, (z // 2) * 3 * plane_count, plane_count, 1)
    pairs = lax.dynamic_slice_in_dim(date_pairs, z * plane_count, plane_count, 0)
    numbers = jnp.arange(dates, dtype=jnp.int32)[None, :]
    pair = ((pairs[:, 1:] == numbers).astype(f32) - (pairs[:, :1] == numbers).astype(f32)).astype(bf16)
    local_count, row_count, col_count = phases.shape
    row_basis = spline_basis(row_count, KNOTS)
    high, low = split(spline_basis(col_count, KNOTS))
    by_row = phases.transpose(1, 0, 2)
    ramp_rows = ramp_call(
        by_row,
        weight_field(coherence).astype(bf16).reshape(row_count, 1, col_count),
        jnp.concatenate([high, low], 1), ramp_inverse, row_basis)
    displacement, residual = line_call(
        by_row, ramp_rows,
        jnp.concatenate([high, low, high], 1).T,
        own, outer, pair)
    return displacement.transpose(1, 0, 2), residual.transpose(1, 0, 2)


def solution(mesh):
    placed = (P("ifg", "strip", None), P("strip", None), P(), P(), P())
    on_line = mesh.shape["ifg"] == PLANE * LINE

    def run(phases, coherence, date_pairs, ramp_inverse, pseudo_inverse):
        dates, ifg_count = pseudo_inverse.shape
        fits = on_line and dates == ifg_count // LINE
        return jax.shard_map(
            per_device_line if fits else per_device,
            mesh=mesh,
            in_specs=placed,
            out_specs=(P(None, ("strip", "ifg"), None), P("ifg", "strip", None)),
            check_vma=False,
        )(phases, coherence, date_pairs, ramp_inverse, pseudo_inverse)

    return run
```

```python
import functools

import jax
import jax.numpy as jnp
from jax import lax
from jax.experimental import pallas as pl
from jax.experimental.pallas import tpu as pltpu
from jax.sharding import PartitionSpec as P

KNOTS = 32
BLOCK = 16
PLANE = 4
LINE = 4
PARTS = 2
LEAD = 3
SKEW = 2
TAIL = 6

highest = lax.Precision.HIGHEST
f32 = jnp.float32
bf16 = jnp.bfloat16


def spline_basis(count, knot_count):
    spacing = (knot_count - 3) / (count - 1)
    places = jnp.arange(count, dtype=jnp.float32) * spacing
    centres = jnp.arange(knot_count, dtype=jnp.float32) - 1.0
    offset = jnp.abs(places[:, None] - centres[None, :])
    inner = 2.0 / 3.0 - offset * offset + 0.5 * offset**3
    outer = (2.0 - offset) ** 3 / 6.0
    return jnp.where(offset < 1.0, inner, jnp.where(offset < 2.0, outer, 0.0))


def weight_field(coherence):
    block_rows, block_cols = coherence.shape
    spread = jnp.broadcast_to(
        coherence.astype(jnp.float32)[:, None, :, None], (block_rows, BLOCK, block_cols, BLOCK)
    )
    return spread.reshape(block_rows * BLOCK, block_cols * BLOCK)


def fit_ramp(phases, coherence, ramp_inverse):
    local_count, row_count, col_count = phases.shape
    square = KNOTS * KNOTS
    row_basis = spline_basis(row_count, KNOTS)
    col_basis = spline_basis(col_count, KNOTS)
    masked = phases.astype(jnp.float32) * weight_field(coherence)
    partial_score = jnp.einsum("irc,cb->irb", masked, col_basis, precision=highest)
    score = jnp.einsum("ra,irb->iab", row_basis, partial_score, precision=highest)
    solved = jnp.dot(
        ramp_inverse.astype(jnp.float32), score.reshape(local_count, square).T, precision=highest
    )
    return solved.T.reshape(local_count, KNOTS, KNOTS), row_basis, col_basis


def per_device(phases, coherence, date_pairs, ramp_inverse, pseudo_inverse):
    row_count = phases.shape[1]
    row_share = row_count // lax.axis_size("ifg")
    coefficients, row_basis, col_basis = fit_ramp(phases, coherence, ramp_inverse)
    ramp_rows = jnp.einsum("ra,iab->irb", row_basis, coefficients, precision=highest)
    ramp = jnp.einsum("irb,cb->irc", ramp_rows, col_basis, precision=highest)
    payload = (phases.astype(jnp.float32) - ramp).astype(jnp.bfloat16)
    regrouped = lax.all_to_all(payload, "ifg", split_axis=1, concat_axis=0, tiled=True)
    total_count, _, col_count = regrouped.shape
    flat = regrouped.reshape(total_count, row_share * col_count)
    displacement = jnp.dot(pseudo_inverse, flat, preferred_element_type=jnp.float32)
    displacement = displacement.reshape(pseudo_inverse.shape[0], row_share, col_count)
    later = jnp.take(displacement, date_pairs[:, 1], axis=0)
    earlier = jnp.take(displacement, date_pairs[:, 0], axis=0)
    residual_band = (regrouped.astype(jnp.float32) - (later - earlier)).astype(jnp.bfloat16)
    residual_phase = lax.all_to_all(residual_band, "ifg", split_axis=0, concat_axis=1, tiled=True)
    return (displacement, residual_phase)


def line_kernel(
    phase_ref, ramp_ref, basis_ref, own_ref, out_ref, pair_ref, disp, resid,
    corr, own_part, out_part, raw, near, far, mid_send, back_send, res_send,
    raw_ss, raw_rs, near_ss, near_rs, far_ss, far_rs, res_ss, res_rs,
):
    rows, count, cols = phase_ref.shape
    chunks, total_count, width = raw.shape
    share = rows // (PLANE * LINE)
    me = lax.axis_index("ifg")
    z = me // PLANE
    q = me % PLANE
    side = z // 2
    inner_z = 1 + side
    outer_z = 3 * side
    is_inner = (z - outer_z) * (1 - 2 * side)
    beside = (inner_z + outer_z - z) * PLANE + q
    partner = (LINE - 1 - z) * PLANE + q
    MESH = pl.DeviceIdType.MESH

    def place(k, owner):
        row = k // PARTS
        return (row // share) * share * PLANE + owner * share + row % share, (k % PARTS) * width

    def peer(p):
        return (q + p) % PLANE

    def raw_copy(k, p):
        return pltpu.make_async_remote_copy(
            src_ref=corr.at[k, peer(p)],
            dst_ref=raw.at[k, pl.ds(pl.multiple_of(q * count, count), count), :],
            send_sem=raw_ss.at[k, p - 1], recv_sem=raw_rs.at[k, p - 1],
            device_id={"ifg": z * PLANE + peer(p)}, device_id_type=MESH)

    def res_copy(k, p):
        row, col = place(k, q)
        return pltpu.make_async_remote_copy(
            src_ref=res_send.at[k, pl.ds(pl.multiple_of(peer(p) * count, count), count), :],
            dst_ref=resid.at[row, :, pl.ds(pl.multiple_of(col, width), width)],
            send_sem=res_ss.at[k, p - 1], recv_sem=res_rs.at[k, p - 1],
            device_id={"ifg": z * PLANE + peer(p)}, device_id_type=MESH)

    def line_copy(src, dst, ss, rs, k, target):
        return pltpu.make_async_remote_copy(
            src_ref=src.at[k], dst_ref=dst.at[k], send_sem=ss.at[k], recv_sem=rs.at[k],
            device_id={"ifg": target}, device_id_type=MESH)

    barrier = pltpu.get_barrier_semaphore()
    for p in range(1, PLANE):
        pl.semaphore_signal(
            barrier, inc=1, device_id={"ifg": z * PLANE + peer(p)}, device_id_type=MESH)
    pl.semaphore_signal(barrier, inc=1, device_id={"ifg": beside}, device_id_type=MESH)

    @pl.when(is_inner == 1)
    def _():
        pl.semaphore_signal(barrier, inc=1, device_id={"ifg": partner}, device_id_type=MESH)

    pl.semaphore_wait(barrier, PLANE + is_inner)

    def dot(a, b):
        return jnp.dot(a, b, preferred_element_type=f32)

    def produce(k):
        part = pl.ds(pl.multiple_of((k % PARTS) * width, width), width)
        lines = ramp_ref[pl.ds((k // PARTS) * PLANE, PLANE)].reshape(PLANE * count, -1)
        ramp = dot(lines, basis_ref[:, part])
        for owner in range(PLANE):
            row, _ = place(k, owner)
            corr[k, owner] = (
                phase_ref[row, :, part].astype(f32) - ramp[owner * count:(owner + 1) * count]
            ).astype(bf16)
        for p in range(1, PLANE):
            raw_copy(k, p).start()
        raw[k, pl.ds(pl.multiple_of(q * count, count), count), :] = corr[k, q]

    @pl.loop(0, LEAD)
    def _(k):
        produce(k)

    def finish(k, total):
        row, col = place(k, q)

        for j in range(share):
            @pl.when(k // PARTS == z * share + j)
            def _():
                disp[:, j, pl.ds(pl.multiple_of(col, width), width)] = total

        high = total.astype(bf16)
        low = (total - high.astype(f32)).astype(bf16)
        modeled = dot(pair_ref[...], high) + dot(pair_ref[...], low)
        res_send[k] = (raw[k].astype(f32) - modeled).astype(bf16)
        for p in range(1, PLANE):
            res_copy(k, p).start()
        resid[row, :, pl.ds(pl.multiple_of(col, width), width)] = res_send[
            k, pl.ds(pl.multiple_of(q * count, count), count), :]

    @pl.loop(0, chunks + TAIL)
    def _(t):
        @pl.when(t + LEAD < chunks)
        def _():
            produce(t + LEAD)

        @pl.when(t < chunks)
        def _():
            k = t
            for p in range(1, PLANE):
                raw_copy(k, p).wait_recv()

            @pl.when(is_inner == 0)
            def _():
                line_copy(raw, near, near_ss, near_rs, k, beside).start()

            @pl.when(is_inner == 1)
            def _():
                line_copy(raw, near, near_ss, near_rs, k, beside).wait_recv()
                slot = k % (SKEW + 1)
                own_sum = dot(own_ref[...], raw[k])
                out_sum = dot(out_ref[...], near[k])
                own_part[slot] = own_sum
                out_part[slot] = out_sum
                mid_send[k] = (own_sum + out_sum).astype(bf16)
                line_copy(mid_send, far, far_ss.at[0], far_rs, k, partner).start()

        @pl.when((is_inner == 1) & (t >= SKEW) & (t < chunks + SKEW))
        def _():
            k = t - SKEW
            line_copy(mid_send, far, far_ss.at[0], far_rs, k, partner).wait_recv()
            slot = k % (SKEW + 1)
            rest = far[k].astype(f32) + own_part[slot]
            back_send[k] = rest.astype(bf16)
            line_copy(back_send, far, far_ss.at[1], far_rs, k, beside).start()
            finish(k, rest + out_part[slot])

        @pl.when((is_inner == 0) & (t >= TAIL))
        def _():
            k = t - TAIL
            line_copy(back_send, far, far_ss.at[1], far_rs, k, beside).wait_recv()
            finish(k, far[k].astype(f32) + dot(own_ref[...], raw[k]))

    @pl.loop(0, chunks)
    def _(k):
        for p in range(1, PLANE):
            raw_copy(k, p).wait_send()
            res_copy(k, p).wait_send()
            res_copy(k, p).wait_recv()

        @pl.when(is_inner == 0)
        def _():
            line_copy(raw, near, near_ss, near_rs, k, beside).wait_send()

        @pl.when(is_inner == 1)
        def _():
            line_copy(mid_send, far, far_ss.at[0], far_rs, k, partner).wait_send()
            line_copy(back_send, far, far_ss.at[1], far_rs, k, beside).wait_send()


def line_call(phases, ramp_rows, basis, own, outer, pair):
    rows, count, cols = phases.shape
    dates, total_count = own.shape
    chunks = rows // PLANE * PARTS
    width = cols // PARTS
    share = rows // (PLANE * LINE)
    slots = pltpu.VMEM((chunks, dates, width), bf16)
    sems = pltpu.SemaphoreType.DMA
    vmem = pl.BlockSpec(memory_space=pltpu.VMEM)
    return pl.pallas_call(
        line_kernel,
        out_shape=(
            jax.ShapeDtypeStruct((dates, share, cols), f32),
            jax.ShapeDtypeStruct((rows, count, cols), bf16),
        ),
        in_specs=[vmem] * 6,
        out_specs=(vmem, vmem),
        scratch_shapes=[pltpu.VMEM((chunks, PLANE, count, width), bf16)] + [pltpu.VMEM((SKEW + 1, dates, width), f32)] * 2 + [slots] * 6 + [
            sems((chunks, PLANE - 1)), sems((chunks, PLANE - 1)),
            sems((chunks,)), sems((chunks,)),
            sems((2, chunks)), sems((chunks,)),
            sems((chunks, PLANE - 1)), sems((chunks, PLANE - 1)),
        ],
        compiler_params=pltpu.CompilerParams(
            collective_id=0, has_side_effects=True, vmem_limit_bytes=52 * 2**20),
        name="line_sums",
    )(phases, ramp_rows, basis, own, outer, pair)


def ramp_kernel(
    phase_ref, weight_ref, basis_ref, inverse_ref, row_ref, rows_out, score, flat, coef,
):
    rows, count, cols = phase_ref.shape
    group = 4

    def first(r):
        return jnp.minimum((r * (KNOTS - 3)) // (rows - 1), KNOTS - 4)

    score[...] = jnp.zeros_like(score)

    @pl.loop(0, rows // group)
    def _(g):
        r0 = g * group
        masked = phase_ref[pl.ds(r0, group)] * weight_ref[pl.ds(r0, group)]
        both = jnp.dot(
            masked.reshape(group * count, cols), basis_ref[...], preferred_element_type=f32)
        part = both[:, :KNOTS] + both[:, KNOTS:]
        for j in range(group):
            base = first(r0 + j)
            for d in range(4):
                score[base + d] += row_ref[r0 + j, base + d] * part[j * count:(j + 1) * count]

    for a in range(KNOTS):
        flat[:, a * KNOTS:(a + 1) * KNOTS] = score[a]
    high = flat[...].astype(bf16)
    low = (flat[...] - high.astype(f32)).astype(bf16)
    across = (((1,), (1,)), ((), ()))
    flat[...] = lax.dot_general(
        high, inverse_ref[...], across, preferred_element_type=f32
    ) + lax.dot_general(low, inverse_ref[...], across, preferred_element_type=f32)
    for a in range(KNOTS):
        coef[a] = flat[:, a * KNOTS:(a + 1) * KNOTS]

    @pl.loop(0, rows // group)
    def _(g):
        for j in range(group):
            r = g * group + j
            base = first(r)
            line = row_ref[r, base] * coef[base]
            for d in range(1, 4):
                line += row_ref[r, base + d] * coef[base + d]
            top = line.astype(bf16)
            rest = (line - top.astype(f32)).astype(bf16)
            share = rows // (PLANE * LINE)
            turn = r // (share * PLANE) * share + r % share
            rows_out[turn * PLANE + r // share % PLANE] = jnp.concatenate([top, top, rest], 1)


def ramp_call(by_row, weight, basis, ramp_inverse, row_basis):
    rows, count, cols = by_row.shape
    vmem = pl.BlockSpec(memory_space=pltpu.VMEM)
    return pl.pallas_call(
        ramp_kernel,
        out_shape=jax.ShapeDtypeStruct((rows, count, 3 * KNOTS), bf16),
        in_specs=[vmem] * 4 + [pl.BlockSpec(memory_space=pltpu.SMEM)],
        out_specs=vmem,
        scratch_shapes=[
            pltpu.VMEM((KNOTS, count, KNOTS), f32),
            pltpu.VMEM((count, KNOTS * KNOTS), f32),
            pltpu.VMEM((KNOTS, count, KNOTS), f32),
        ],
        compiler_params=pltpu.CompilerParams(vmem_limit_bytes=32 * 2**20),
        name="ramp_fit",
    )(by_row, weight, basis, ramp_inverse, row_basis)


def split(values):
    high = lax.reduce_precision(values, exponent_bits=8, mantissa_bits=7)
    return high.astype(bf16), (values - high).astype(bf16)


def per_device_line(phases, coherence, date_pairs, ramp_inverse, pseudo_inverse):
    dates, ifg_count = pseudo_inverse.shape
    plane_count = ifg_count // LINE
    z = lax.axis_index("ifg") // PLANE
    own = lax.dynamic_slice_in_dim(pseudo_inverse, z * plane_count, plane_count, 1)
    outer = lax.dynamic_slice_in_dim(pseudo_inverse, (z // 2) * 3 * plane_count, plane_count, 1)
    pairs = lax.dynamic_slice_in_dim(date_pairs, z * plane_count, plane_count, 0)
    numbers = jnp.arange(dates, dtype=jnp.int32)[None, :]
    pair = ((pairs[:, 1:] == numbers).astype(f32) - (pairs[:, :1] == numbers).astype(f32)).astype(bf16)
    local_count, row_count, col_count = phases.shape
    row_basis = spline_basis(row_count, KNOTS)
    high, low = split(spline_basis(col_count, KNOTS))
    by_row = phases.transpose(1, 0, 2)
    ramp_rows = ramp_call(
        by_row,
        weight_field(coherence).astype(bf16).reshape(row_count, 1, col_count),
        jnp.concatenate([high, low], 1), ramp_inverse, row_basis)
    displacement, residual = line_call(
        by_row, ramp_rows,
        jnp.concatenate([high, low, high], 1).T,
        own, outer, pair)
    return displacement, residual.transpose(1, 0, 2)


def solution(mesh):
    placed = (P("ifg", "strip", None), P("strip", None), P(), P(), P())
    on_line = mesh.shape["ifg"] == PLANE * LINE

    def run(phases, coherence, date_pairs, ramp_inverse, pseudo_inverse):
        dates, ifg_count = pseudo_inverse.shape
        fits = on_line and dates == ifg_count // LINE
        return jax.shard_map(
            per_device_line if fits else per_device,
            mesh=mesh,
            in_specs=placed,
            out_specs=(P(None, ("strip", "ifg"), None), P("ifg", "strip", None)),
            check_vma=False,
        )(phases, coherence, date_pairs, ramp_inverse, pseudo_inverse)

    return run
```

```python
import functools

import jax
import jax.numpy as jnp
from jax import lax
from jax.experimental import pallas as pl
from jax.experimental.pallas import tpu as pltpu
from jax.sharding import PartitionSpec as P

KNOTS = 32
BLOCK = 16
PLANE = 4
LINE = 4
PARTS = 2
LEAD = 2
SKEW = 2
TAIL = 5

highest = lax.Precision.HIGHEST
f32 = jnp.float32
bf16 = jnp.bfloat16


def spline_basis(count, knot_count):
    spacing = (knot_count - 3) / (count - 1)
    places = jnp.arange(count, dtype=jnp.float32) * spacing
    centres = jnp.arange(knot_count, dtype=jnp.float32) - 1.0
    offset = jnp.abs(places[:, None] - centres[None, :])
    inner = 2.0 / 3.0 - offset * offset + 0.5 * offset**3
    outer = (2.0 - offset) ** 3 / 6.0
    return jnp.where(offset < 1.0, inner, jnp.where(offset < 2.0, outer, 0.0))


def weight_field(coherence):
    block_rows, block_cols = coherence.shape
    spread = jnp.broadcast_to(
        coherence.astype(jnp.float32)[:, None, :, None], (block_rows, BLOCK, block_cols, BLOCK)
    )
    return spread.reshape(block_rows * BLOCK, block_cols * BLOCK)


def fit_ramp(phases, coherence, ramp_inverse):
    local_count, row_count, col_count = phases.shape
    square = KNOTS * KNOTS
    row_basis = spline_basis(row_count, KNOTS)
    col_basis = spline_basis(col_count, KNOTS)
    masked = phases.astype(jnp.float32) * weight_field(coherence)
    partial_score = jnp.einsum("irc,cb->irb", masked, col_basis, precision=highest)
    score = jnp.einsum("ra,irb->iab", row_basis, partial_score, precision=highest)
    solved = jnp.dot(
        ramp_inverse.astype(jnp.float32), score.reshape(local_count, square).T, precision=highest
    )
    return solved.T.reshape(local_count, KNOTS, KNOTS), row_basis, col_basis


def per_device(phases, coherence, date_pairs, ramp_inverse, pseudo_inverse):
    row_count = phases.shape[1]
    row_share = row_count // lax.axis_size("ifg")
    coefficients, row_basis, col_basis = fit_ramp(phases, coherence, ramp_inverse)
    ramp_rows = jnp.einsum("ra,iab->irb", row_basis, coefficients, precision=highest)
    ramp = jnp.einsum("irb,cb->irc", ramp_rows, col_basis, precision=highest)
    payload = (phases.astype(jnp.float32) - ramp).astype(jnp.bfloat16)
    regrouped = lax.all_to_all(payload, "ifg", split_axis=1, concat_axis=0, tiled=True)
    total_count, _, col_count = regrouped.shape
    flat = regrouped.reshape(total_count, row_share * col_count)
    displacement = jnp.dot(pseudo_inverse, flat, preferred_element_type=jnp.float32)
    displacement = displacement.reshape(pseudo_inverse.shape[0], row_share, col_count)
    later = jnp.take(displacement, date_pairs[:, 1], axis=0)
    earlier = jnp.take(displacement, date_pairs[:, 0], axis=0)
    residual_band = (regrouped.astype(jnp.float32) - (later - earlier)).astype(jnp.bfloat16)
    residual_phase = lax.all_to_all(residual_band, "ifg", split_axis=0, concat_axis=1, tiled=True)
    return (displacement, residual_phase)


def line_kernel(
    phase_ref, ramp_ref, basis_ref, own_ref, out_ref, pair_ref, disp, resid,
    corr, own_part, out_part, raw, near, far, mid_send, back_send, res_send,
    raw_ss, raw_rs, near_ss, near_rs, far_ss, far_rs, res_ss, res_rs,
):
    rows, count, cols = phase_ref.shape
    chunks, total_count, width = raw.shape
    share = rows // (PLANE * LINE)
    me = lax.axis_index("ifg")
    z = me // PLANE
    q = me % PLANE
    side = z // 2
    inner_z = 1 + side
    outer_z = 3 * side
    is_inner = (z - outer_z) * (1 - 2 * side)
    beside = (inner_z + outer_z - z) * PLANE + q
    partner = (LINE - 1 - z) * PLANE + q
    MESH = pl.DeviceIdType.MESH

    def place(k, owner):
        row = k // PARTS
        return (row // share) * share * PLANE + owner * share + row % share, (k % PARTS) * width

    def peer(p):
        return (q + p) % PLANE

    def raw_copy(k, p):
        return pltpu.make_async_remote_copy(
            src_ref=corr.at[k, peer(p)],
            dst_ref=raw.at[k, pl.ds(pl.multiple_of(q * count, count), count), :],
            send_sem=raw_ss.at[k, p - 1], recv_sem=raw_rs.at[k, p - 1],
            device_id={"ifg": z * PLANE + peer(p)}, device_id_type=MESH)

    def res_copy(k, p):
        row, col = place(k, q)
        return pltpu.make_async_remote_copy(
            src_ref=res_send.at[k, pl.ds(pl.multiple_of(peer(p) * count, count), count), :],
            dst_ref=resid.at[row, :, pl.ds(pl.multiple_of(col, width), width)],
            send_sem=res_ss.at[k, p - 1], recv_sem=res_rs.at[k, p - 1],
            device_id={"ifg": z * PLANE + peer(p)}, device_id_type=MESH)

    def line_copy(src, dst, ss, rs, k, target):
        return pltpu.make_async_remote_copy(
            src_ref=src.at[k], dst_ref=dst.at[k], send_sem=ss.at[k], recv_sem=rs.at[k],
            device_id={"ifg": target}, device_id_type=MESH)

    barrier = pltpu.get_barrier_semaphore()
    for p in range(1, PLANE):
        pl.semaphore_signal(
            barrier, inc=1, device_id={"ifg": z * PLANE + peer(p)}, device_id_type=MESH)
    pl.semaphore_signal(barrier, inc=1, device_id={"ifg": beside}, device_id_type=MESH)

    @pl.when(is_inner == 1)
    def _():
        pl.semaphore_signal(barrier, inc=1, device_id={"ifg": partner}, device_id_type=MESH)

    pl.semaphore_wait(barrier, PLANE + is_inner)

    def dot(a, b):
        return jnp.dot(a, b, preferred_element_type=f32)

    def produce(k):
        part = pl.ds(pl.multiple_of((k % PARTS) * width, width), width)
        lines = ramp_ref[pl.ds((k // PARTS) * PLANE, PLANE)].reshape(PLANE * count, -1)
        ramp = dot(lines, basis_ref[:, part])
        for owner in range(PLANE):
            row, _ = place(k, owner)
            corr[k, owner] = (
                phase_ref[row, :, part].astype(f32) - ramp[owner * count:(owner + 1) * count]
            ).astype(bf16)
        for p in range(1, PLANE):
            raw_copy(k, p).start()
        raw[k, pl.ds(pl.multiple_of(q * count, count), count), :] = corr[k, q]

    @pl.loop(0, LEAD)
    def _(k):
        produce(k)

    def finish(k, total):
        row, col = place(k, q)

        for j in range(share):
            @pl.when(k // PARTS == z * share + j)
            def _():
                disp[:, j, pl.ds(pl.multiple_of(col, width), width)] = total

        high = total.astype(bf16)
        low = (total - high.astype(f32)).astype(bf16)
        modeled = dot(pair_ref[...], high) + dot(pair_ref[...], low)
        res_send[k] = (raw[k].astype(f32) - modeled).astype(bf16)
        for p in range(1, PLANE):
            res_copy(k, p).start()
        resid[row, :, pl.ds(pl.multiple_of(col, width), width)] = res_send[
            k, pl.ds(pl.multiple_of(q * count, count), count), :]

    @pl.loop(0, chunks + TAIL)
    def _(t):
        @pl.when(t + LEAD < chunks)
        def _():
            produce(t + LEAD)

        @pl.when(t < chunks)
        def _():
            k = t
            for p in range(1, PLANE):
                raw_copy(k, p).wait_recv()

            @pl.when(is_inner == 0)
            def _():
                line_copy(raw, near, near_ss, near_rs, k, beside).start()

            @pl.when(is_inner == 1)
            def _():
                line_copy(raw, near, near_ss, near_rs, k, beside).wait_recv()
                slot = k % (SKEW + 1)
                own_sum = dot(own_ref[...], raw[k])
                out_sum = dot(out_ref[...], near[k])
                own_part[slot] = own_sum
                out_part[slot] = out_sum
                mid_send[k] = (own_sum + out_sum).astype(bf16)
                line_copy(mid_send, far, far_ss.at[0], far_rs, k, partner).start()

        @pl.when((is_inner == 1) & (t >= SKEW) & (t < chunks + SKEW))
        def _():
            k = t - SKEW
            line_copy(mid_send, far, far_ss.at[0], far_rs, k, partner).wait_recv()
            slot = k % (SKEW + 1)
            rest = far[k].astype(f32) + own_part[slot]
            back_send[k] = rest.astype(bf16)
            line_copy(back_send, far, far_ss.at[1], far_rs, k, beside).start()
            finish(k, rest + out_part[slot])

        @pl.when((is_inner == 0) & (t >= TAIL))
        def _():
            k = t - TAIL
            line_copy(back_send, far, far_ss.at[1], far_rs, k, beside).wait_recv()
            finish(k, far[k].astype(f32) + dot(own_ref[...], raw[k]))

    @pl.loop(0, chunks)
    def _(k):
        for p in range(1, PLANE):
            raw_copy(k, p).wait_send()
            res_copy(k, p).wait_send()
            res_copy(k, p).wait_recv()

        @pl.when(is_inner == 0)
        def _():
            line_copy(raw, near, near_ss, near_rs, k, beside).wait_send()

        @pl.when(is_inner == 1)
        def _():
            line_copy(mid_send, far, far_ss.at[0], far_rs, k, partner).wait_send()
            line_copy(back_send, far, far_ss.at[1], far_rs, k, beside).wait_send()


def line_call(phases, ramp_rows, basis, own, outer, pair):
    rows, count, cols = phases.shape
    dates, total_count = own.shape
    chunks = rows // PLANE * PARTS
    width = cols // PARTS
    share = rows // (PLANE * LINE)
    slots = pltpu.VMEM((chunks, dates, width), bf16)
    sems = pltpu.SemaphoreType.DMA
    vmem = pl.BlockSpec(memory_space=pltpu.VMEM)
    return pl.pallas_call(
        line_kernel,
        out_shape=(
            jax.ShapeDtypeStruct((dates, share, cols), f32),
            jax.ShapeDtypeStruct((rows, count, cols), bf16),
        ),
        in_specs=[vmem] * 6,
        out_specs=(vmem, vmem),
        scratch_shapes=[pltpu.VMEM((chunks, PLANE, count, width), bf16)] + [pltpu.VMEM((SKEW + 1, dates, width), f32)] * 2 + [slots] * 6 + [
            sems((chunks, PLANE - 1)), sems((chunks, PLANE - 1)),
            sems((chunks,)), sems((chunks,)),
            sems((2, chunks)), sems((chunks,)),
            sems((chunks, PLANE - 1)), sems((chunks, PLANE - 1)),
        ],
        compiler_params=pltpu.CompilerParams(
            collective_id=0, has_side_effects=True, vmem_limit_bytes=52 * 2**20),
        name="line_sums",
    )(phases, ramp_rows, basis, own, outer, pair)


def ramp_kernel(
    phase_ref, weight_ref, basis_ref, inverse_ref, row_ref, rows_out, score, flat, coef,
):
    rows, count, cols = phase_ref.shape
    group = 4

    def first(r):
        return jnp.minimum((r * (KNOTS - 3)) // (rows - 1), KNOTS - 4)

    score[...] = jnp.zeros_like(score)

    @pl.loop(0, rows // group)
    def _(g):
        r0 = g * group
        masked = phase_ref[pl.ds(r0, group)] * weight_ref[pl.ds(r0, group)]
        both = jnp.dot(
            masked.reshape(group * count, cols), basis_ref[...], preferred_element_type=f32)
        part = both[:, :KNOTS] + both[:, KNOTS:]
        for j in range(group):
            base = first(r0 + j)
            for d in range(4):
                score[base + d] += row_ref[r0 + j, base + d] * part[j * count:(j + 1) * count]

    for a in range(KNOTS):
        flat[:, a * KNOTS:(a + 1) * KNOTS] = score[a]
    high = flat[...].astype(bf16)
    low = (flat[...] - high.astype(f32)).astype(bf16)
    across = (((1,), (1,)), ((), ()))
    flat[...] = lax.dot_general(
        high, inverse_ref[...], across, preferred_element_type=f32
    ) + lax.dot_general(low, inverse_ref[...], across, preferred_element_type=f32)
    for a in range(KNOTS):
        coef[a] = flat[:, a * KNOTS:(a + 1) * KNOTS]

    @pl.loop(0, rows // group)
    def _(g):
        for j in range(group):
            r = g * group + j
            base = first(r)
            line = row_ref[r, base] * coef[base]
            for d in range(1, 4):
                line += row_ref[r, base + d] * coef[base + d]
            top = line.astype(bf16)
            rest = (line - top.astype(f32)).astype(bf16)
            share = rows // (PLANE * LINE)
            turn = r // (share * PLANE) * share + r % share
            rows_out[turn * PLANE + r // share % PLANE] = jnp.concatenate([top, top, rest], 1)


def ramp_call(by_row, weight, basis, ramp_inverse, row_basis):
    rows, count, cols = by_row.shape
    vmem = pl.BlockSpec(memory_space=pltpu.VMEM)
    return pl.pallas_call(
        ramp_kernel,
        out_shape=jax.ShapeDtypeStruct((rows, count, 3 * KNOTS), bf16),
        in_specs=[vmem] * 4 + [pl.BlockSpec(memory_space=pltpu.SMEM)],
        out_specs=vmem,
        scratch_shapes=[
            pltpu.VMEM((KNOTS, count, KNOTS), f32),
            pltpu.VMEM((count, KNOTS * KNOTS), f32),
            pltpu.VMEM((KNOTS, count, KNOTS), f32),
        ],
        compiler_params=pltpu.CompilerParams(vmem_limit_bytes=32 * 2**20),
        name="ramp_fit",
    )(by_row, weight, basis, ramp_inverse, row_basis)


def split(values):
    high = lax.reduce_precision(values, exponent_bits=8, mantissa_bits=7)
    return high.astype(bf16), (values - high).astype(bf16)


def per_device_line(phases, coherence, date_pairs, ramp_inverse, pseudo_inverse):
    dates, ifg_count = pseudo_inverse.shape
    plane_count = ifg_count // LINE
    z = lax.axis_index("ifg") // PLANE
    own = lax.dynamic_slice_in_dim(pseudo_inverse, z * plane_count, plane_count, 1)
    outer = lax.dynamic_slice_in_dim(pseudo_inverse, (z // 2) * 3 * plane_count, plane_count, 1)
    pairs = lax.dynamic_slice_in_dim(date_pairs, z * plane_count, plane_count, 0)
    numbers = jnp.arange(dates, dtype=jnp.int32)[None, :]
    pair = ((pairs[:, 1:] == numbers).astype(f32) - (pairs[:, :1] == numbers).astype(f32)).astype(bf16)
    local_count, row_count, col_count = phases.shape
    row_basis = spline_basis(row_count, KNOTS)
    high, low = split(spline_basis(col_count, KNOTS))
    by_row = phases.transpose(1, 0, 2)
    ramp_rows = ramp_call(
        by_row,
        weight_field(coherence).astype(bf16).reshape(row_count, 1, col_count),
        jnp.concatenate([high, low], 1), ramp_inverse, row_basis)
    displacement, residual = line_call(
        by_row, ramp_rows,
        jnp.concatenate([high, low, high], 1).T,
        own, outer, pair)
    return displacement, residual.transpose(1, 0, 2)


def solution(mesh):
    placed = (P("ifg", "strip", None), P("strip", None), P(), P(), P())
    on_line = mesh.shape["ifg"] == PLANE * LINE

    def run(phases, coherence, date_pairs, ramp_inverse, pseudo_inverse):
        dates, ifg_count = pseudo_inverse.shape
        fits = on_line and dates == ifg_count // LINE
        return jax.shard_map(
            per_device_line if fits else per_device,
            mesh=mesh,
            in_specs=placed,
            out_specs=(P(None, ("strip", "ifg"), None), P("ifg", "strip", None)),
            check_vma=False,
        )(phases, coherence, date_pairs, ramp_inverse, pseudo_inverse)

    return run
```
